32 devices in a mesh: rx: 8 (over y, x, core), ry: 4 (over z).
Axes of the slice: x: 2, y: 2, z: 4, core: 2. Of those that a mesh axis runs over, the one named last changes fastest.
Arguments:
- rhs: float32 [4096, 128], P(('rx', 'ry')), may hold values from -6 to 6
- a_diag: bfloat16 [4096, 128, 128], P(('rx', 'ry'))
- a_pair: bfloat16 [4096, 128, 128], P(('rx', 'ry')), may hold values from -0.25 to 0.25
- a_far: bfloat16 [4096, 2, 128, 128], P(('rx', 'ry')), may hold values from -0.25 to 0.25
- approx_inv: bfloat16 [4096, 128, 128], P(('rx', 'ry'))
- prolong: bfloat16 [4096, 128, 128], P(('rx', 'ry'))
- col_index: int32 [4096, 2], P(('rx', 'ry')), may hold values from 0 to 4095, as said below
- partner: int32 [2048], P(('rx', 'ry')), may hold values from 1 to 4095, as said below
- odd_owner: int32 [2048], P(('rx', 'ry')), may hold values from 0 to 2047, as said below
Outputs:
- fine: float32 [4096, 128], P(('rx', 'ry'))
- coarse_blocks: bfloat16 [2048, 128, 128], P(('rx', 'ry'))
- coarse_residual: float32 [2048, 128], P(('rx', 'ry'))
The draws below stay inside these ranges and needn't reach their ends.
Inputs may be any that keep to these rules, and one draw needn't show every extreme that they name: partner[c] is an odd fine row on another device with the same ry index as coarse row c's device (coarse row c stands on device c // 64, fine row i on device i // 128); every odd fine row is named once; the odd rows of each device go to exactly 4 devices, 16 rows to each. odd_owner[o] is the coarse row c with partner[c] = 2o + 1. col_index[i,0] is a block row of a device with the same ry index as row i's device; col_index[i,1] a block row of the device with the same rx index whose ry index is one more or one less, wrapping.
All inputs are finite; a program needn't handle non-finite values.
Results may differ from the reference program's by a relative error of at most 0.0065.
Values may be sent and summed in bfloat16 or wider, within the bound.
A program may use at most 128 MiB of HBM per device.

```python
import math
import jax
import jax.numpy as jnp
from jax import lax

B = 128
BR_DEV = 128
SWEEPS = 2
OFFS = 4
CR_DEV = 64
CAP = 16
NB = 4096
NC = 2048
N_RX = 8
N_RY = 4


def noise_blocks(key):
    return jax.random.normal(key, (NB, B, B), jnp.float32)


def matched(key):
    base_key = jax.random.fold_in(key, 7)
    devices = N_RX * N_RY
    key_set = jax.random.split(base_key, 3)
    line_keys = jax.random.split(key_set[0], N_RY)
    offsets = jax.vmap(lambda item_key: jax.random.permutation(item_key, N_RX - 1))(line_keys).astype(jnp.int32)[:, :OFFS] + 1
    source_order = jax.vmap(lambda item_key: jax.random.permutation(item_key, CR_DEV))(jax.random.split(key_set[1], devices)).astype(jnp.int32)
    slot_order = jax.vmap(lambda item_key: jax.random.permutation(item_key, CR_DEV))(jax.random.split(key_set[2], devices)).astype(jnp.int32)
    device_ids = jnp.arange(devices, dtype=jnp.int32)[:, None]
    line_index = device_ids // N_RY
    column_index = device_ids % N_RY
    group_index = slot_order // CAP
    rank_index = slot_order % CAP
    source_line = (line_index - offsets[column_index, group_index]) % N_RX
    source_dev = source_line * N_RY + column_index
    local_odd = source_order[source_dev, group_index * CAP + rank_index]
    partner_ids = (source_dev * BR_DEV + 2 * local_odd + 1).reshape(-1).astype(jnp.int32)
    coarse_ids = (device_ids * CR_DEV + jnp.arange(CR_DEV, dtype=jnp.int32)[None, :]).reshape(-1).astype(jnp.int32)
    owner_ids = jnp.zeros((NC,), jnp.int32).at[(source_dev * CR_DEV + local_odd).reshape(-1)].set(coarse_ids)
    return (partner_ids, owner_ids)


def draw_partner(key, part):
    return matched(key)[0]


def draw_odd_owner(key, part):
    return matched(key)[1]


def draw_col_index(key, part):
    key_set = jax.random.split(jax.random.fold_in(key, 11), 4)
    row_ids = jnp.arange(NB, dtype=jnp.int32)
    device_ids = row_ids // BR_DEV
    line_index = device_ids // N_RY
    column_index = device_ids % N_RY
    far_line = jax.random.randint(key_set[0], (NB,), 0, N_RX, jnp.int32)
    far_local = jax.random.randint(key_set[1], (NB,), 0, BR_DEV, jnp.int32)
    first_col = (far_line * N_RY + column_index) * BR_DEV + far_local
    direction = jax.random.randint(key_set[2], (NB,), 0, 2, jnp.int32) * 2 - 1
    side_column = (column_index + direction) % N_RY
    side_local = jax.random.randint(key_set[3], (NB,), 0, BR_DEV, jnp.int32)
    second_col = (line_index * N_RY + side_column) * BR_DEV + side_local
    return jnp.stack([first_col, second_col], axis=1).astype(jnp.int32)


def draw_a_diag(key, part):
    key_set = jax.random.split(jax.random.fold_in(key, 21), 2)
    scales = jax.random.uniform(key_set[1], (NB, B), jnp.float32, 3.5, 5.0)
    identity = jnp.eye(B, dtype=jnp.float32)
    return (noise_blocks(key_set[0]) / B ** 0.5 + identity[None, :, :] * scales[:, :, None]).astype(jnp.bfloat16)


def draw_approx_inv(key, part):
    identity = jnp.eye(B, dtype=jnp.float32)
    return (0.25 * identity[None, :, :] + 0.08 * noise_blocks(jax.random.fold_in(key, 31)) / B ** 0.5).astype(jnp.bfloat16)


def draw_prolong(key, part):
    identity = jnp.eye(B, dtype=jnp.float32)
    return (identity[None, :, :] + 0.5 * noise_blocks(jax.random.fold_in(key, 41)) / B ** 0.5).astype(jnp.bfloat16)


def steps_of(own_key, extent, cuts, least, top_value):
    factor_of, own = 1.0, jax.random.fold_in(own_key, 6)
    for position, shards_of in cuts:
        heights = jnp.exp(jax.random.uniform(jax.random.fold_in(own, position), (shards_of,), jnp.float32, least / len(cuts), top_value / len(cuts)))
        factor_of = factor_of * jnp.repeat(heights, extent[position] // shards_of).reshape([-1 if axis == position else 1 for axis in range(len(extent))])
    return factor_of


def bell_draw(key, extent, scale, reach, cuts=(), held_as=jnp.bfloat16):
    drawn = jax.random.normal(key, extent, jnp.float32) * scale
    if len(cuts) > 0:
        drawn = steps_of(key, extent, cuts, -0.22, 0.18) * drawn
    return jnp.clip(drawn, min=-reach, max=reach).astype(held_as)


def setup_inputs(seed: int = 0) -> dict:
    seeds = jax.random.split(jax.random.key(seed), 10)
    rhs = bell_draw(seeds[0], (NB, B), 1.0, 6.0, ((0, 32),), jnp.float32)
    a_diag = draw_a_diag(jax.random.fold_in(seeds[9], 71), 0)
    a_pair = bell_draw(seeds[2], (NB, B, B), (4 * B) ** -0.5, 0.25, ((0, 32),))
    a_far = bell_draw(seeds[3], (NB, 2, B, B), (4 * B) ** -0.5, 0.25, ((0, 32),))
    approx_inv = draw_approx_inv(jax.random.fold_in(seeds[9], 71), 0)
    prolong = draw_prolong(jax.random.fold_in(seeds[9], 71), 0)
    col_index = draw_col_index(jax.random.fold_in(seeds[9], 71), 0)
    partner = draw_partner(jax.random.fold_in(seeds[9], 71), 0)
    odd_owner = draw_odd_owner(jax.random.fold_in(seeds[9], 71), 0)
    return dict(rhs=rhs, a_diag=a_diag, a_pair=a_pair, a_far=a_far, approx_inv=approx_inv, prolong=prolong, col_index=col_index, partner=partner, odd_owner=odd_owner)


OMEGA = 0.7
THETA = 0.08


def mat_vec(matrix, vector):
    return jnp.einsum('nij,nj->ni', matrix.astype(jnp.float32), vector, precision=lax.Precision.HIGHEST)


def mat_tvec(matrix, vector):
    return jnp.einsum('nji,nj->ni', matrix.astype(jnp.float32), vector, precision=lax.Precision.HIGHEST)


def mat_mat(left_mat, right_mat):
    return jnp.einsum('nij,njk->nik', left_mat.astype(jnp.float32), right_mat.astype(jnp.float32), precision=lax.Precision.HIGHEST)


def mat_tmat(left_mat, right_mat):
    return jnp.einsum('nji,njk->nik', left_mat.astype(jnp.float32), right_mat.astype(jnp.float32), precision=lax.Precision.HIGHEST)


def rounded(values):
    return lax.optimization_barrier(values.astype(jnp.bfloat16))


def by_groups(function, amount):
    group_size = math.gcd(amount, 256)
    indices = jnp.arange(amount, dtype=jnp.int32).reshape(amount // group_size, group_size)
    mapped = lax.map(function, indices)
    return jax.tree.map(lambda tensor: tensor.reshape((amount,) + tensor.shape[2:]), mapped)


def reference(rhs, a_diag, a_pair, a_far, approx_inv, prolong, col_index, partner, odd_owner):
    mate = jnp.stack([partner, 2 * odd_owner], axis=1).reshape(NB).astype(jnp.int32)

    def operate(vector):
        def row_terms(indices):
            total = mat_vec(a_diag[indices], vector[indices])
            total = total + mat_vec(a_pair[indices], vector[mate[indices]])
            total = total + mat_vec(a_far[indices, 0], vector[col_index[indices, 0]])
            return total + mat_vec(a_far[indices, 1], vector[col_index[indices, 1]])
        return by_groups(row_terms, NB)

    iterate = jnp.zeros((NB, B), jnp.float32)
    for sweep_index in range(SWEEPS):
        defect = rhs - operate(iterate)
        iterate = iterate + OMEGA * by_groups(lambda indices: mat_vec(approx_inv[indices], defect[indices]), NB)
    residual = rhs - operate(iterate)

    def coarse_rows(indices):
        even_rows = 2 * indices
        odd_rows = partner[indices]
        first_map = prolong[even_rows]
        second_map = prolong[odd_rows]
        upper = rounded(mat_tmat(first_map, a_diag[even_rows]))
        across = rounded(mat_tmat(first_map, a_pair[even_rows]))
        lower = rounded(mat_tmat(second_map, a_diag[odd_rows]))
        behind = rounded(mat_tmat(second_map, a_pair[odd_rows]))
        inner = rounded(mat_mat(lower, second_map))
        total = mat_mat(upper, first_map) + mat_mat(across, second_map) + mat_mat(behind, first_map) + inner.astype(jnp.float32)
        blocks = rounded(total)
        restricted = mat_tvec(first_map, residual[even_rows]) + mat_tvec(second_map, residual[odd_rows])
        correction = THETA * restricted
        correction = correction + THETA * (restricted - mat_vec(blocks, correction))
        return blocks, restricted, mat_vec(first_map, correction), mat_vec(second_map, correction)

    blocks, restricted, lift_even, lift_odd = by_groups(coarse_rows, NC)
    even_ids = 2 * jnp.arange(NC, dtype=jnp.int32)
    fine = iterate.at[even_ids].add(lift_even).at[partner].add(lift_odd)
    return fine, blocks, restricted
```

```python
import functools

import jax
import jax.numpy as jnp
from jax import lax
from jax.experimental import pallas as pl
from jax.experimental.pallas import tpu as pltpu
from jax.sharding import PartitionSpec as P

OMEGA = 0.7
THETA = 0.08
MESH = pl.DeviceIdType.MESH
BF = jnp.bfloat16
F32 = jnp.float32

NT = (((1,), (1,)), ((), ()))
NN = (((1,), (0,)), ((), ()))
TN = (((0,), (0,)), ((), ()))


def dot(left, right, dims):
    return lax.dot_general(left, right, dims, preferred_element_type=F32)


def two_parts(values):
    high = values.astype(BF)
    low = (values - high.astype(F32)).astype(BF)
    return jnp.concatenate([high, low], axis=0)


def kernel(
    n,
    m,
    cap,
    rows,
    idx,
    rhs,
    h_diag,
    h_pair,
    h_far,
    h_inv,
    h_prol,
    fine_out,
    h_blocks,
    rest_out,
    v_diag,
    v_pair,
    v_far,
    v_inv,
    v_prol,
    out_blocks,
    send_p,
    send_b,
    send_i,
    recv_p,
    recv_b,
    recv_i,
    pre,
    it_send,
    it_recv,
    side_recv,
    line_vals,
    side_vals,
    mate_rows,
    far_rows,
    side_rows,
    iterate,
    defect,
    restr,
    corr,
    odd_corr,
    piece_send,
    piece_recv,
    back_send,
    back_recv,
    load_sems,
    s_sems,
    r_sems,
    ss_sems,
    sr_sems,
):
    half = rows // 2
    slots = (n - 1) * cap
    mate_at, far_at, side_at = 0, rows, 2 * rows
    recv_at = 3 * rows
    send_at = recv_at + half
    item_at = send_at + half
    back_at = item_at + slots
    line = lax.axis_index("rx")
    col = lax.axis_index("ry")
    peers = [lax.rem(line + o, n) for o in range(1, n)]
    back_peers = [lax.rem(line + n - o, n) for o in range(1, n)]
    below, above = lax.rem(col + m - 1, m), lax.rem(col + 1, m)

    loads = [
        pltpu.make_async_copy(src, dst, load_sems.at[i])
        for i, (src, dst) in enumerate(
            [(h_inv, v_inv), (h_prol, v_prol), (h_diag, v_diag), (h_pair, v_pair), (h_far, v_far)]
        )
    ]
    for load in loads:
        load.start()

    barrier = pltpu.get_barrier_semaphore()
    for peer in peers:
        pl.semaphore_signal(barrier, inc=1, device_id=(peer, col), device_id_type=MESH)
    for side in (below, above):
        pl.semaphore_signal(barrier, inc=1, device_id=(line, side), device_id_type=MESH)
    pl.semaphore_wait(barrier, n + 1)

    def to_peer(kind, o, src, dst, back=False):
        return pltpu.make_async_remote_copy(
            src_ref=src,
            dst_ref=dst,
            send_sem=s_sems.at[kind, o],
            recv_sem=r_sems.at[kind, o],
            device_id=((back_peers if back else peers)[o], col),
            device_id_type=MESH,
        )

    def iterate_copies(turn):
        copies = [
            to_peer(turn, o, it_send.at[turn], it_recv.at[turn, o]) for o in range(n - 1)
        ]
        for k, side in enumerate((above, below)):
            copies.append(
                pltpu.make_async_remote_copy(
                    src_ref=it_send.at[turn],
                    dst_ref=side_recv.at[turn, k],
                    send_sem=ss_sems.at[turn, k],
                    recv_sem=sr_sems.at[turn, k],
                    device_id=(line, side),
                    device_id_type=MESH,
                )
            )
        return copies

    row_id = lax.broadcasted_iota(jnp.int32, (8, 128), 0)

    def groups(count, body):
        def step(g, carry):
            body(pl.multiple_of(g * 8, 8))
            return carry

        lax.fori_loop(0, count // 8, step, 0)

    def exact_rows(values, first, matrix, dims):
        both = two_parts(values)
        total = jnp.zeros((8, 128), F32)
        for r in range(8):
            part = dot(both, matrix(first + r), dims)
            total = jnp.where(row_id == r, part[:8] + part[8:], total)
        return total

    def gather_rows(turn):
        line_vals[0] = it_send[turn].astype(F32)
        for o in range(n - 1):
            line_vals[o + 1] = it_recv[turn, o].astype(F32)
        side_vals[...] = side_recv[turn].astype(F32)

        def step(g, carry):
            for r in range(8):
                i = g * 8 + r
                a = idx[mate_at + i]
                b = idx[far_at + i]
                c = idx[side_at + i]
                mate_rows[pl.ds(i, 1), :] = line_vals[a // rows, pl.ds(a % rows, 1), :]
                far_rows[pl.ds(i, 1), :] = line_vals[b // rows, pl.ds(b % rows, 1), :]
                side_rows[pl.ds(i, 1), :] = side_vals[c // rows, pl.ds(c % rows, 1), :]
            return carry

        lax.fori_loop(0, rows // 8, step, 0)

    def subtract_operator():
        def body(first):
            at = pl.ds(first, 8)
            own = two_parts(iterate[at, :])
            mates = mate_rows[at, :].astype(BF)
            fars = far_rows[at, :].astype(BF)
            sides = side_rows[at, :].astype(BF)
            total = jnp.zeros((8, 128), F32)
            for r in range(8):
                i = first + r
                main = dot(own, v_diag[i], NT)
                part = main[:8] + main[8:] + dot(mates, v_pair[i], NT)
                part = part + dot(fars, v_far[i, 0], NT) + dot(sides, v_far[i, 1], NT)
                total = jnp.where(row_id == r, part, total)
            defect[at, :] = rhs[at, :] - total

        groups(rows, body)

    loads[0].wait()

    def first_sweep(first):
        at = pl.ds(first, 8)
        iterate[at, :] = OMEGA * exact_rows(rhs[at, :], first, lambda i: v_inv[i], NT)

    groups(rows, first_sweep)
    it_send[0] = iterate[...].astype(BF)
    it_copies = iterate_copies(0)
    for copy in it_copies:
        copy.start()

    loads[1].wait()
    p_copies = []
    for o in range(n - 1):

        def pack(k, carry):
            send_p[o, k] = v_prol[2 * idx[item_at + o * cap + k] + 1]
            return carry

        lax.fori_loop(0, cap, pack, 0)
        p_copies.append(to_peer(2, o, send_p.at[o], recv_p.at[o]))
        p_copies[-1].start()

    for load in loads[2:]:
        load.wait()
    for copy in it_copies:
        copy.wait()
    gather_rows(0)
    subtract_operator()

    def second_sweep(first):
        at = pl.ds(first, 8)
        step = exact_rows(defect[at, :], first, lambda i: v_inv[i], NT)
        iterate[at, :] = iterate[at, :] + OMEGA * step

    groups(rows, second_sweep)
    it_send[1] = iterate[...].astype(BF)
    it_copies = iterate_copies(1)
    for copy in it_copies:
        copy.start()

    b_copies = []
    for o in range(n - 1):

        def behind(k, carry):
            i = 2 * idx[item_at + o * cap + k] + 1
            send_b[o, k] = dot(v_prol[i], v_pair[i], TN).astype(BF)
            return carry

        lax.fori_loop(0, cap, behind, 0)
        b_copies.append(to_peer(3, o, send_b.at[o], recv_b.at[o]))
        b_copies[-1].start()

    i_copies = []
    for o in range(n - 1):

        def inner(k, carry):
            i = 2 * idx[item_at + o * cap + k] + 1
            block = v_prol[i]
            lower = dot(block, v_diag[i], TN).astype(BF)
            send_i[o, k] = dot(lower, block, NN).astype(BF)
            return carry

        lax.fori_loop(0, cap, inner, 0)
        i_copies.append(to_peer(4, o, send_i.at[o], recv_i.at[o]))

    for copy in it_copies:
        copy.wait()
    gather_rows(1)
    subtract_operator()

    def restrict(first):
        at = pl.ds(first, 8)
        mate_rows[at, :] = exact_rows(defect[at, :], first, lambda i: v_prol[i], NN)

    groups(rows, restrict)
    piece_copies = []
    for o in range(n - 1):
        for k in range(cap):
            i = 2 * idx[item_at + o * cap + k] + 1
            piece_send[o, pl.ds(k, 1), :] = mate_rows[pl.ds(i, 1), :]
        piece_copies.append(to_peer(5, o, piece_send.at[o], piece_recv.at[o]))
        piece_copies[-1].start()
    for copy in i_copies:
        copy.start()

    for copy in p_copies:
        copy.wait()
    for copy in b_copies:
        copy.wait()

    def products(c, carry):
        slot = idx[recv_at + c]
        block = v_prol[2 * c]
        upper = dot(block, v_diag[2 * c], TN).astype(BF)
        across = dot(block, v_pair[2 * c], TN).astype(BF)
        total = dot(upper, block, NN)
        total = total + dot(across, recv_p[slot // cap, slot % cap], NN)
        pre[c] = total + dot(recv_b[slot // cap, slot % cap], block, NN)
        return carry

    lax.fori_loop(0, half, products, 0)

    for copy in piece_copies:
        copy.wait()

    def restricted(g, carry):
        for r in range(8):
            c = g * 8 + r
            slot = idx[recv_at + c]
            piece = piece_recv[slot // cap, pl.ds(slot % cap, 1), :]
            restr[pl.ds(c, 1), :] = mate_rows[pl.ds(2 * c, 1), :] + piece
        return carry

    lax.fori_loop(0, half // 8, restricted, 0)
    rest_out[...] = restr[...]

    for copy in i_copies:
        copy.wait()

    def finish(c, carry):
        slot = idx[recv_at + c]
        last = recv_i[slot // cap, slot % cap].astype(F32)
        out_blocks[c] = (pre[c] + last).astype(BF)
        return carry

    lax.fori_loop(0, half, finish, 0)
    store = pltpu.make_async_copy(out_blocks, h_blocks, load_sems.at[5])
    store.start()

    def correct(first):
        at = pl.ds(first, 8)
        value = restr[at, :]
        start = THETA * value
        moved = exact_rows(start, first, lambda c: out_blocks[c], NT)
        corr[at, :] = start + THETA * (value - moved)

    groups(half, correct)
    back_copies = []
    for o in range(n - 1):
        for k in range(cap):
            c = idx[back_at + o * cap + k]
            back_send[o, pl.ds(k, 1), :] = corr[pl.ds(c, 1), :]
        back_copies.append(to_peer(6, o, back_send.at[o], back_recv.at[o], back=True))
        back_copies[-1].start()

    def lift_even(first):
        at = pl.ds(first, 8)
        odd_corr[at, :] = exact_rows(corr[at, :], first, lambda c: v_prol[2 * c], NT)
        for r in range(8):
            i = 2 * (first + r)
            fine_out[pl.ds(i, 1), :] = iterate[pl.ds(i, 1), :] + odd_corr[pl.ds(first + r, 1), :]

    groups(half, lift_even)
    for copy in back_copies:
        copy.wait()

    def take_back(g, carry):
        for r in range(8):
            j = g * 8 + r
            slot = idx[send_at + j]
            odd_corr[pl.ds(j, 1), :] = back_recv[slot // cap, pl.ds(slot % cap, 1), :]
        return carry

    lax.fori_loop(0, half // 8, take_back, 0)

    def lift_odd(first):
        at = pl.ds(first, 8)
        corr[at, :] = exact_rows(odd_corr[at, :], first, lambda j: v_prol[2 * j + 1], NT)
        for r in range(8):
            i = 2 * (first + r) + 1
            fine_out[pl.ds(i, 1), :] = iterate[pl.ds(i, 1), :] + corr[pl.ds(first + r, 1), :]

    groups(half, lift_odd)
    store.wait()


def tables(n, m, cap, rows, col_index, partner, odd_owner):
    half = rows // 2
    slots = (n - 1) * cap
    line = lax.axis_index("rx")
    col = lax.axis_index("ry")
    mate = jnp.stack([partner, 2 * odd_owner], axis=1).reshape(rows)

    def line_slot(row):
        return (line - row // rows // m) % n * rows + row % rows

    below = (col_index[:, 1] // rows) % m == (col - 1) % m
    side = jnp.where(below, 0, rows) + col_index[:, 1] % rows
    order = jnp.arange(half, dtype=jnp.int32)

    def slot_of(offset, key):
        same = offset[:, None] == offset[None, :]
        rank = jnp.sum(same & (key[None, :] < key[:, None]), axis=1, dtype=jnp.int32)
        return (offset - 1) * cap + rank

    send = slot_of((odd_owner // half // m - line) % n, odd_owner)
    recv = slot_of((line - partner // rows // m) % n, order)

    def inverse(slot):
        hits = slot[None, :] == jnp.arange(slots, dtype=jnp.int32)[:, None]
        return jnp.sum(jnp.where(hits, order[None, :], 0), axis=1, dtype=jnp.int32)

    return jnp.concatenate(
        [line_slot(mate), line_slot(col_index[:, 0]), side, recv, send, inverse(send), inverse(recv)]
    )


def body(n, m, rhs, a_diag, a_pair, a_far, approx_inv, prolong, col_index, partner, odd_owner):
    rows, width = rhs.shape
    half = rows // 2
    cap = half // (n // 2)
    idx = tables(n, m, cap, rows, col_index, partner, odd_owner)
    vmem = pl.BlockSpec(memory_space=pltpu.VMEM)
    hbm = pl.BlockSpec(memory_space=pl.ANY)
    block = (width, width)
    slot_blocks = pltpu.VMEM((n - 1, cap) + block, BF)
    row_vals = pltpu.VMEM((rows, width), F32)
    half_vals = pltpu.VMEM((half, width), F32)
    slot_vals = pltpu.VMEM((n - 1, cap, width), F32)
    row_blocks = pltpu.VMEM((rows,) + block, BF)
    dma = pltpu.SemaphoreType.DMA
    fine, blocks, restricted = pl.pallas_call(
        functools.partial(kernel, n, m, cap, rows),
        out_shape=(
            jax.ShapeDtypeStruct((rows, width), F32),
            jax.ShapeDtypeStruct((half,) + block, BF),
            jax.ShapeDtypeStruct((half, width), F32),
        ),
        in_specs=[pl.BlockSpec(memory_space=pltpu.SMEM), vmem] + [hbm] * 5,
        out_specs=(vmem, hbm, vmem),
        scratch_shapes=[
            row_blocks,
            row_blocks,
            pltpu.VMEM((rows, 2) + block, BF),
            row_blocks,
            row_blocks,
            pltpu.VMEM((half,) + block, BF),
            slot_blocks,
            slot_blocks,
            slot_blocks,
            slot_blocks,
            slot_blocks,
            slot_blocks,
            pltpu.VMEM((half,) + block, F32),
            pltpu.VMEM((2, rows, width), BF),
            pltpu.VMEM((2, n - 1, rows, width), BF),
            pltpu.VMEM((2, 2, rows, width), BF),
            pltpu.VMEM((n, rows, width), F32),
            pltpu.VMEM((2, rows, width), F32),
            row_vals,
            row_vals,
            row_vals,
            row_vals,
            row_vals,
            half_vals,
            half_vals,
            half_vals,
            slot_vals,
            slot_vals,
            slot_vals,
            slot_vals,
            dma((6,)),
            dma((7, n - 1)),
            dma((7, n - 1)),
            dma((2, 2)),
            dma((2, 2)),
        ],
        compiler_params=pltpu.CompilerParams(
            collective_id=0, has_side_effects=True, vmem_limit_bytes=61 * 1024 * 1024
        ),
    )(idx, rhs, a_diag, a_pair, a_far, approx_inv, prolong)
    return (fine, blocks, restricted)


def solution(mesh):
    n, m = mesh.shape["rx"], mesh.shape["ry"]
    return jax.shard_map(
        functools.partial(body, n, m),
        mesh=mesh,
        in_specs=(
            P(("rx", "ry"), None),
            P(("rx", "ry"), None, None),
            P(("rx", "ry"), None, None),
            P(("rx", "ry"), None, None, None),
            P(("rx", "ry"), None, None),
            P(("rx", "ry"), None, None),
            P(("rx", "ry"), None),
            P(("rx", "ry")),
            P(("rx", "ry")),
        ),
        out_specs=(P(("rx", "ry"), None), P(("rx", "ry"), None, None), P(("rx", "ry"), None)),
        check_vma=False,
    )
```

```python
import functools

import jax
import jax.numpy as jnp
from jax import lax
from jax.experimental import pallas as pl
from jax.experimental.pallas import tpu as pltpu
from jax.sharding import PartitionSpec as P

OMEGA = 0.7
THETA = 0.08
MESH = pl.DeviceIdType.MESH
BF = jnp.bfloat16
F32 = jnp.float32

NT = (((1,), (1,)), ((), ()))
NN = (((1,), (0,)), ((), ()))
TN = (((0,), (0,)), ((), ()))


def dot(left, right, dims):
    return lax.dot_general(left, right, dims, preferred_element_type=F32)


def two_parts(values):
    high = values.astype(BF)
    low = (values - high.astype(F32)).astype(BF)
    return jnp.concatenate([high, low], axis=0)


def kernel(
    n,
    m,
    cap,
    rows,
    idx,
    rhs,
    h_diag,
    h_pair,
    h_far,
    h_inv,
    h_prol,
    fine_out,
    h_blocks,
    rest_out,
    v_diag,
    v_pair,
    v_far,
    v_inv,
    v_prol,
    out_blocks,
    send_p,
    send_b,
    send_i,
    recv_p,
    recv_b,
    recv_i,
    pre,
    it_send,
    it_recv,
    side_recv,
    line_vals,
    side_vals,
    mate_rows,
    far_rows,
    side_rows,
    iterate,
    defect,
    restr,
    corr,
    odd_corr,
    piece_send,
    piece_recv,
    back_send,
    back_recv,
    load_sems,
    s_sems,
    r_sems,
    ss_sems,
    sr_sems,
):
    half = rows // 2
    slots = (n - 1) * cap
    mate_at, far_at, side_at = 0, rows, 2 * rows
    recv_at = 3 * rows
    send_at = recv_at + half
    item_at = send_at + half
    back_at = item_at + slots
    line = lax.axis_index("rx")
    col = lax.axis_index("ry")
    peers = [lax.rem(line + o, n) for o in range(1, n)]
    back_peers = [lax.rem(line + n - o, n) for o in range(1, n)]
    below, above = lax.rem(col + m - 1, m), lax.rem(col + 1, m)

    loads = [
        pltpu.make_async_copy(src, dst, load_sems.at[i])
        for i, (src, dst) in enumerate(
            [(h_prol, v_prol), (h_inv, v_inv), (h_pair, v_pair), (h_diag, v_diag), (h_far, v_far)]
        )
    ]
    for load in loads:
        load.start()

    barrier = pltpu.get_barrier_semaphore()
    for peer in peers:
        pl.semaphore_signal(barrier, inc=1, device_id=(peer, col), device_id_type=MESH)
    for side in (below, above):
        pl.semaphore_signal(barrier, inc=1, device_id=(line, side), device_id_type=MESH)
    def to_peer(kind, o, src, dst, back=False):
        return pltpu.make_async_remote_copy(
            src_ref=src,
            dst_ref=dst,
            send_sem=s_sems.at[kind, o],
            recv_sem=r_sems.at[kind, o],
            device_id=((back_peers if back else peers)[o], col),
            device_id_type=MESH,
        )

    def iterate_copies(turn):
        copies = [
            to_peer(turn, o, it_send.at[turn], it_recv.at[turn, o]) for o in range(n - 1)
        ]
        for k, side in enumerate((above, below)):
            copies.append(
                pltpu.make_async_remote_copy(
                    src_ref=it_send.at[turn],
                    dst_ref=side_recv.at[turn, k],
                    send_sem=ss_sems.at[turn, k],
                    recv_sem=sr_sems.at[turn, k],
                    device_id=(line, side),
                    device_id_type=MESH,
                )
            )
        return copies

    row_id = lax.broadcasted_iota(jnp.int32, (8, 128), 0)

    def groups(count, body):
        def step(g, carry):
            body(pl.multiple_of(g * 8, 8))
            return carry

        lax.fori_loop(0, count // 8, step, 0)

    def exact_rows(values, first, matrix, dims):
        both = two_parts(values)
        total = jnp.zeros((8, 128), F32)
        for r in range(8):
            part = dot(both, matrix(first + r), dims)
            total = jnp.where(row_id == r, part[:8] + part[8:], total)
        return total

    def gather_rows(turn):
        line_vals[0] = it_send[turn].astype(F32)
        for o in range(n - 1):
            line_vals[o + 1] = it_recv[turn, o].astype(F32)
        side_vals[...] = side_recv[turn].astype(F32)

        def step(g, carry):
            for r in range(8):
                i = g * 8 + r
                a = idx[mate_at + i]
                b = idx[far_at + i]
                c = idx[side_at + i]
                mate_rows[pl.ds(i, 1), :] = line_vals[a // rows, pl.ds(a % rows, 1), :]
                far_rows[pl.ds(i, 1), :] = line_vals[b // rows, pl.ds(b % rows, 1), :]
                side_rows[pl.ds(i, 1), :] = side_vals[c // rows, pl.ds(c % rows, 1), :]
            return carry

        lax.fori_loop(0, rows // 8, step, 0)

    def subtract_operator():
        def body(first):
            at = pl.ds(first, 8)
            own = two_parts(iterate[at, :])
            mates = mate_rows[at, :].astype(BF)
            fars = far_rows[at, :].astype(BF)
            sides = side_rows[at, :].astype(BF)
            total = jnp.zeros((8, 128), F32)
            for r in range(8):
                i = first + r
                main = dot(own, v_diag[i], NT)
                part = main[:8] + main[8:] + dot(mates, v_pair[i], NT)
                part = part + dot(fars, v_far[i, 0], NT) + dot(sides, v_far[i, 1], NT)
                total = jnp.where(row_id == r, part, total)
            defect[at, :] = rhs[at, :] - total

        groups(rows, body)

    loads[0].wait()
    for o in range(n - 1):

        def pack(k, carry):
            for r in range(4):
                send_p[o, 4 * k + r] = v_prol[2 * idx[item_at + o * cap + 4 * k + r] + 1]
            return carry

        lax.fori_loop(0, cap // 4, pack, 0)
    pl.semaphore_wait(barrier, n + 1)
    p_copies = [to_peer(2, o, send_p.at[o], recv_p.at[o]) for o in range(n - 1)]
    for copy in p_copies:
        copy.start()

    loads[1].wait()

    def first_sweep(first):
        at = pl.ds(first, 8)
        iterate[at, :] = OMEGA * exact_rows(rhs[at, :], first, lambda i: v_inv[i], NT)

    groups(rows, first_sweep)
    it_send[0] = iterate[...].astype(BF)
    it_copies = iterate_copies(0)
    for copy in it_copies:
        copy.start()

    loads[2].wait()
    b_copies = []
    for o in range(n - 1):

        def behind(k, carry):
            for r in range(4):
                i = 2 * idx[item_at + o * cap + 4 * k + r] + 1
                send_b[o, 4 * k + r] = dot(v_prol[i], v_pair[i], TN).astype(BF)
            return carry

        lax.fori_loop(0, cap // 4, behind, 0)
        b_copies.append(to_peer(3, o, send_b.at[o], recv_b.at[o]))
        b_copies[-1].start()

    for load in loads[3:]:
        load.wait()
    for copy in it_copies:
        copy.wait()
    gather_rows(0)
    subtract_operator()

    def second_sweep(first):
        at = pl.ds(first, 8)
        step = exact_rows(defect[at, :], first, lambda i: v_inv[i], NT)
        iterate[at, :] = iterate[at, :] + OMEGA * step

    groups(rows, second_sweep)
    it_send[1] = iterate[...].astype(BF)
    it_copies = iterate_copies(1)
    for copy in it_copies:
        copy.start()

    i_copies = []
    for o in range(n - 1):

        def inner(k, carry):
            for r in range(4):
                i = 2 * idx[item_at + o * cap + 4 * k + r] + 1
                block = v_prol[i]
                lower = dot(block, v_diag[i], TN).astype(BF)
                send_i[o, 4 * k + r] = dot(lower, block, NN).astype(BF)
            return carry

        lax.fori_loop(0, cap // 4, inner, 0)
        i_copies.append(to_peer(4, o, send_i.at[o], recv_i.at[o]))
        i_copies[-1].start()

    for copy in it_copies:
        copy.wait()
    gather_rows(1)
    subtract_operator()

    def restrict(first):
        at = pl.ds(first, 8)
        mate_rows[at, :] = exact_rows(defect[at, :], first, lambda i: v_prol[i], NN)

    groups(rows, restrict)
    piece_copies = []
    for o in range(n - 1):
        for k in range(cap):
            i = 2 * idx[item_at + o * cap + k] + 1
            piece_send[o, pl.ds(k, 1), :] = mate_rows[pl.ds(i, 1), :]
        piece_copies.append(to_peer(5, o, piece_send.at[o], piece_recv.at[o]))
        piece_copies[-1].start()

    for copy in p_copies:
        copy.wait()
    for copy in b_copies:
        copy.wait()

    def products(g, carry):
        for r in range(4):
            c = 4 * g + r
            slot = idx[recv_at + c]
            block = v_prol[2 * c]
            upper = dot(block, v_diag[2 * c], TN).astype(BF)
            across = dot(block, v_pair[2 * c], TN).astype(BF)
            total = dot(upper, block, NN)
            total = total + dot(across, recv_p[slot // cap, slot % cap], NN)
            pre[c] = total + dot(recv_b[slot // cap, slot % cap], block, NN)
        return carry

    lax.fori_loop(0, half // 4, products, 0)

    for copy in piece_copies:
        copy.wait()

    def restricted(g, carry):
        for r in range(8):
            c = g * 8 + r
            slot = idx[recv_at + c]
            piece = piece_recv[slot // cap, pl.ds(slot % cap, 1), :]
            restr[pl.ds(c, 1), :] = mate_rows[pl.ds(2 * c, 1), :] + piece
        return carry

    lax.fori_loop(0, half // 8, restricted, 0)
    rest_out[...] = restr[...]

    for copy in i_copies:
        copy.wait()

    def finish(first):
        at = pl.ds(first, 8)
        value = restr[at, :]
        start = THETA * value
        both = two_parts(start)
        moved = jnp.zeros((8, 128), F32)
        for r in range(8):
            slot = idx[recv_at + first + r]
            last = recv_i[slot // cap, slot % cap].astype(F32)
            made = (pre[first + r] + last).astype(BF)
            out_blocks[first + r] = made
            part = dot(both, made, NT)
            moved = jnp.where(row_id == r, part[:8] + part[8:], moved)
        corr[at, :] = start + THETA * (value - moved)

    groups(half, finish)
    store = pltpu.make_async_copy(out_blocks, h_blocks, load_sems.at[5])
    store.start()
    back_copies = []
    for o in range(n - 1):
        for k in range(cap):
            c = idx[back_at + o * cap + k]
            back_send[o, pl.ds(k, 1), :] = corr[pl.ds(c, 1), :]
        back_copies.append(to_peer(6, o, back_send.at[o], back_recv.at[o], back=True))
        back_copies[-1].start()

    def lift_even(first):
        at = pl.ds(first, 8)
        odd_corr[at, :] = exact_rows(corr[at, :], first, lambda c: v_prol[2 * c], NT)
        for r in range(8):
            i = 2 * (first + r)
            fine_out[pl.ds(i, 1), :] = iterate[pl.ds(i, 1), :] + odd_corr[pl.ds(first + r, 1), :]

    groups(half, lift_even)
    for copy in back_copies:
        copy.wait()

    def take_back(g, carry):
        for r in range(8):
            j = g * 8 + r
            slot = idx[send_at + j]
            odd_corr[pl.ds(j, 1), :] = back_recv[slot // cap, pl.ds(slot % cap, 1), :]
        return carry

    lax.fori_loop(0, half // 8, take_back, 0)

    def lift_odd(first):
        at = pl.ds(first, 8)
        corr[at, :] = exact_rows(odd_corr[at, :], first, lambda j: v_prol[2 * j + 1], NT)
        for r in range(8):
            i = 2 * (first + r) + 1
            fine_out[pl.ds(i, 1), :] = iterate[pl.ds(i, 1), :] + corr[pl.ds(first + r, 1), :]

    groups(half, lift_odd)
    store.wait()


def hand_over(fine, blocks, rest, fine_out, blocks_out, rest_out, sems):
    count = sems.shape[0] - 2
    size = blocks.shape[0] // count
    copies = [
        pltpu.make_async_copy(
            blocks.at[pl.ds(k * size, size)], blocks_out.at[pl.ds(k * size, size)], sems.at[k]
        )
        for k in range(count)
    ]
    copies.append(pltpu.make_async_copy(fine, fine_out, sems.at[count]))
    copies.append(pltpu.make_async_copy(rest, rest_out, sems.at[count + 1]))
    for copy in copies:
        copy.start()
    for copy in copies:
        copy.wait()


def tables(n, m, cap, rows, col_index, partner, odd_owner):
    half = rows // 2
    slots = (n - 1) * cap
    line = lax.axis_index("rx")
    col = lax.axis_index("ry")
    mate = jnp.stack([partner, 2 * odd_owner], axis=1).reshape(rows)

    def line_slot(row):
        return (line - row // rows // m) % n * rows + row % rows

    below = (col_index[:, 1] // rows) % m == (col - 1) % m
    side = jnp.where(below, 0, rows) + col_index[:, 1] % rows
    order = jnp.arange(half, dtype=jnp.int32)

    def slot_of(offset, key):
        same = offset[:, None] == offset[None, :]
        rank = jnp.sum(same & (key[None, :] < key[:, None]), axis=1, dtype=jnp.int32)
        return (offset - 1) * cap + rank

    send = slot_of((odd_owner // half // m - line) % n, odd_owner)
    recv = slot_of((line - partner // rows // m) % n, order)

    def inverse(slot):
        hits = slot[None, :] == jnp.arange(slots, dtype=jnp.int32)[:, None]
        return jnp.sum(jnp.where(hits, order[None, :], 0), axis=1, dtype=jnp.int32)

    return jnp.concatenate(
        [line_slot(mate), line_slot(col_index[:, 0]), side, recv, send, inverse(send), inverse(recv)]
    )


def body(n, m, rhs, a_diag, a_pair, a_far, approx_inv, prolong, col_index, partner, odd_owner):
    rows, width = rhs.shape
    half = rows // 2
    cap = half // (n // 2)
    idx = tables(n, m, cap, rows, col_index, partner, odd_owner)
    vmem = pl.BlockSpec(memory_space=pltpu.VMEM)
    hbm = pl.BlockSpec(memory_space=pl.ANY)
    block = (width, width)
    slot_blocks = pltpu.VMEM((n - 1, cap) + block, BF)
    row_vals = pltpu.VMEM((rows, width), F32)
    half_vals = pltpu.VMEM((half, width), F32)
    slot_vals = pltpu.VMEM((n - 1, cap, width), F32)
    row_blocks = pltpu.VMEM((rows,) + block, BF)
    dma = pltpu.SemaphoreType.DMA
    fine, blocks, restricted = pl.pallas_call(
        functools.partial(kernel, n, m, cap, rows),
        out_shape=(
            jax.ShapeDtypeStruct((rows, width), F32),
            jax.ShapeDtypeStruct((half,) + block, BF),
            jax.ShapeDtypeStruct((half, width), F32),
        ),
        in_specs=[pl.BlockSpec(memory_space=pltpu.SMEM), vmem] + [hbm] * 5,
        out_specs=(vmem, hbm, vmem),
        scratch_shapes=[
            row_blocks,
            row_blocks,
            pltpu.VMEM((rows, 2) + block, BF),
            row_blocks,
            row_blocks,
            pltpu.VMEM((half,) + block, BF),
            slot_blocks,
            slot_blocks,
            slot_blocks,
            slot_blocks,
            slot_blocks,
            slot_blocks,
            pltpu.VMEM((half,) + block, F32),
            pltpu.VMEM((2, rows, width), BF),
            pltpu.VMEM((2, n - 1, rows, width), BF),
            pltpu.VMEM((2, 2, rows, width), BF),
            pltpu.VMEM((n, rows, width), F32),
            pltpu.VMEM((2, rows, width), F32),
            row_vals,
            row_vals,
            row_vals,
            row_vals,
            row_vals,
            half_vals,
            half_vals,
            half_vals,
            slot_vals,
            slot_vals,
            slot_vals,
            slot_vals,
            dma((6,)),
            dma((7, n - 1)),
            dma((7, n - 1)),
            dma((2, 2)),
            dma((2, 2)),
        ],
        compiler_params=pltpu.CompilerParams(
            collective_id=0, has_side_effects=True, vmem_limit_bytes=61 * 1024 * 1024
        ),
    )(idx, rhs, a_diag, a_pair, a_far, approx_inv, prolong)
    return pl.pallas_call(
        hand_over,
        out_shape=[jax.ShapeDtypeStruct(a.shape, a.dtype) for a in (fine, blocks, restricted)],
        in_specs=[hbm] * 3,
        out_specs=[hbm] * 3,
        scratch_shapes=[dma((10,))],
    )(fine, blocks, restricted)


def solution(mesh):
    n, m = mesh.shape["rx"], mesh.shape["ry"]
    return jax.shard_map(
        functools.partial(body, n, m),
        mesh=mesh,
        in_specs=(
            P(("rx", "ry"), None),
            P(("rx", "ry"), None, None),
            P(("rx", "ry"), None, None),
            P(("rx", "ry"), None, None, None),
            P(("rx", "ry"), None, None),
            P(("rx", "ry"), None, None),
            P(("rx", "ry"), None),
            P(("rx", "ry")),
            P(("rx", "ry")),
        ),
        out_specs=(P(("rx", "ry"), None), P(("rx", "ry"), None, None), P(("rx", "ry"), None)),
        check_vma=False,
    )
```

```python
import functools

import jax
import jax.numpy as jnp
from jax import lax
from jax.experimental import pallas as pl
from jax.experimental.pallas import tpu as pltpu
from jax.sharding import PartitionSpec as P

OMEGA = 0.7
THETA = 0.08
MESH = pl.DeviceIdType.MESH
BF = jnp.bfloat16
F32 = jnp.float32

NT = (((1,), (1,)), ((), ()))
NN = (((1,), (0,)), ((), ()))
TN = (((0,), (0,)), ((), ()))


def dot(left, right, dims):
    return lax.dot_general(left, right, dims, preferred_element_type=F32)


def two_parts(values):
    high = values.astype(BF)
    low = (values - high.astype(F32)).astype(BF)
    return jnp.concatenate([high, low], axis=0)


def kernel(
    n,
    m,
    cap,
    rows,
    idx,
    rhs,
    h_diag,
    h_pair,
    h_far,
    h_inv,
    h_prol,
    fine_out,
    h_blocks,
    rest_out,
    v_diag,
    v_pair,
    v_far,
    v_inv,
    v_prol,
    out_blocks,
    send_p,
    send_b,
    send_i,
    recv_p,
    recv_b,
    recv_i,
    pre,
    it_send,
    it_recv,
    side_recv,
    line_vals,
    side_vals,
    mate_rows,
    far_rows,
    side_rows,
    iterate,
    defect,
    restr,
    corr,
    odd_corr,
    piece_send,
    piece_recv,
    back_send,
    back_recv,
    load_sems,
    s_sems,
    r_sems,
    ss_sems,
    sr_sems,
):
    half = rows // 2
    slots = (n - 1) * cap
    mate_at, far_at, side_at = 0, rows, 2 * rows
    recv_at = 3 * rows
    send_at = recv_at + half
    item_at = send_at + half
    back_at = item_at + slots
    line = lax.axis_index("rx")
    col = lax.axis_index("ry")
    peers = [lax.rem(line + o, n) for o in range(1, n)]
    back_peers = [lax.rem(line + n - o, n) for o in range(1, n)]
    below, above = lax.rem(col + m - 1, m), lax.rem(col + 1, m)

    loads = [
        pltpu.make_async_copy(src, dst, load_sems.at[i])
        for i, (src, dst) in enumerate(
            [(h_prol, v_prol), (h_inv, v_inv), (h_pair, v_pair), (h_diag, v_diag), (h_far, v_far)]
        )
    ]
    for load in loads:
        load.start()

    barrier = pltpu.get_barrier_semaphore()
    for peer in peers:
        pl.semaphore_signal(barrier, inc=1, device_id=(peer, col), device_id_type=MESH)
    for side in (below, above):
        pl.semaphore_signal(barrier, inc=1, device_id=(line, side), device_id_type=MESH)
    def to_peer(kind, o, src, dst, back=False):
        return pltpu.make_async_remote_copy(
            src_ref=src,
            dst_ref=dst,
            send_sem=s_sems.at[kind, o],
            recv_sem=r_sems.at[kind, o],
            device_id=((back_peers if back else peers)[o], col),
            device_id_type=MESH,
        )

    turn_to = 1 - 2 * lax.rem(line, 2)
    twin = line + turn_to

    def iterate_copy(turn, src, dst_at, sem_at, peer):
        return pltpu.make_async_remote_copy(
            src_ref=src,
            dst_ref=it_recv.at[turn, dst_at],
            send_sem=s_sems.at[turn, sem_at],
            recv_sem=r_sems.at[turn, dst_at],
            device_id=(peer, col),
            device_id_type=MESH,
        )

    twin_at = lax.rem(turn_to + n, n) - 1
    twin_from = lax.rem(n - turn_to, n) - 1

    def send_iterate(turn):
        copies = [iterate_copy(turn, it_send.at[turn], twin_at, 0, twin)]
        for o in range(2, n, 2):
            copies.append(iterate_copy(turn, it_send.at[turn], o - 1, o - 1, peers[o - 1]))
        for k, side in enumerate((above, below)):
            copies.append(
                pltpu.make_async_remote_copy(
                    src_ref=it_send.at[turn],
                    dst_ref=side_recv.at[turn, k],
                    send_sem=ss_sems.at[turn, k],
                    recv_sem=sr_sems.at[turn, k],
                    device_id=(line, side),
                    device_id_type=MESH,
                )
            )
        for copy in copies:
            copy.start()
        return copies

    def take_iterates(turn, copies):
        passed = []
        for o in range(2, n, 2):
            copies[o // 2].wait_recv()
            dst_at = lax.rem(o + turn_to + n, n) - 1
            passed.append(iterate_copy(turn, it_recv.at[turn, o - 1], dst_at, o, twin))
            passed[-1].start()
        for copy in copies:
            copy.wait_send()
        for copy in copies[n // 2 :]:
            copy.wait_recv()
        iterate_copy(turn, it_send.at[turn], twin_from, 0, twin).wait_recv()
        for o in range(2, n, 2):
            source_at = lax.rem(o - turn_to + n, n) - 1
            iterate_copy(turn, it_send.at[turn], source_at, o, twin).wait_recv()
        for copy in passed:
            copy.wait_send()

    row_id = lax.broadcasted_iota(jnp.int32, (8, 128), 0)

    def groups(count, body):
        def step(g, carry):
            body(pl.multiple_of(g * 8, 8))
            return carry

        lax.fori_loop(0, count // 8, step, 0)

    def exact_rows(values, first, matrix, dims):
        both = two_parts(values)
        total = jnp.zeros((8, 128), F32)
        for r in range(8):
            part = dot(both, matrix(first + r), dims)
            total = jnp.where(row_id == r, part[:8] + part[8:], total)
        return total

    def gather_rows(turn):
        line_vals[0] = it_send[turn].astype(F32)
        for o in range(n - 1):
            line_vals[o + 1] = it_recv[turn, o].astype(F32)
        side_vals[...] = side_recv[turn].astype(F32)

        def step(g, carry):
            for r in range(8):
                i = g * 8 + r
                a = idx[mate_at + i]
                b = idx[far_at + i]
                c = idx[side_at + i]
                mate_rows[pl.ds(i, 1), :] = line_vals[a // rows, pl.ds(a % rows, 1), :]
                far_rows[pl.ds(i, 1), :] = line_vals[b // rows, pl.ds(b % rows, 1), :]
                side_rows[pl.ds(i, 1), :] = side_vals[c // rows, pl.ds(c % rows, 1), :]
            return carry

        lax.fori_loop(0, rows // 8, step, 0)

    def subtract_operator():
        def body(first):
            at = pl.ds(first, 8)
            own = two_parts(iterate[at, :])
            mates = mate_rows[at, :].astype(BF)
            fars = far_rows[at, :].astype(BF)
            sides = side_rows[at, :].astype(BF)
            total = jnp.zeros((8, 128), F32)
            for r in range(8):
                i = first + r
                main = dot(own, v_diag[i], NT)
                part = main[:8] + main[8:] + dot(mates, v_pair[i], NT)
                part = part + dot(fars, v_far[i, 0], NT) + dot(sides, v_far[i, 1], NT)
                total = jnp.where(row_id == r, part, total)
            defect[at, :] = rhs[at, :] - total

        groups(rows, body)

    loads[0].wait()
    pl.semaphore_wait(barrier, n + 1)
    p_copies = []
    for o in range(n - 1):

        def pack(k, carry):
            for r in range(4):
                send_p[o, 4 * k + r] = v_prol[2 * idx[item_at + o * cap + 4 * k + r] + 1]
            return carry

        lax.fori_loop(0, cap // 4, pack, 0)
        p_copies.append(to_peer(2, o, send_p.at[o], recv_p.at[o]))
        p_copies[-1].start()

    loads[1].wait()

    def first_sweep(first):
        at = pl.ds(first, 8)
        iterate[at, :] = OMEGA * exact_rows(rhs[at, :], first, lambda i: v_inv[i], NT)

    groups(rows, first_sweep)
    it_send[0] = iterate[...].astype(BF)
    it_copies = send_iterate(0)

    loads[2].wait()
    b_copies = []
    for o in range(n - 1):

        def behind(k, carry):
            for r in range(4):
                i = 2 * idx[item_at + o * cap + 4 * k + r] + 1
                send_b[o, 4 * k + r] = dot(v_prol[i], v_pair[i], TN).astype(BF)
            return carry

        lax.fori_loop(0, cap // 4, behind, 0)
        b_copies.append(to_peer(3, o, send_b.at[o], recv_b.at[o]))
        b_copies[-1].start()

    for load in loads[3:]:
        load.wait()
    take_iterates(0, it_copies)
    gather_rows(0)
    subtract_operator()

    def second_sweep(first):
        at = pl.ds(first, 8)
        step = exact_rows(defect[at, :], first, lambda i: v_inv[i], NT)
        iterate[at, :] = iterate[at, :] + OMEGA * step

    groups(rows, second_sweep)
    it_send[1] = iterate[...].astype(BF)
    it_copies = send_iterate(1)

    i_copies = []
    for o in range(n - 1):

        def inner(k, carry):
            for r in range(4):
                i = 2 * idx[item_at + o * cap + 4 * k + r] + 1
                block = v_prol[i]
                lower = dot(block, v_diag[i], TN).astype(BF)
                send_i[o, 4 * k + r] = dot(lower, block, NN).astype(BF)
            return carry

        lax.fori_loop(0, cap // 4, inner, 0)
        i_copies.append(to_peer(4, o, send_i.at[o], recv_i.at[o]))
        i_copies[-1].start()

    take_iterates(1, it_copies)
    gather_rows(1)
    subtract_operator()

    def restrict(first):
        at = pl.ds(first, 8)
        mate_rows[at, :] = exact_rows(defect[at, :], first, lambda i: v_prol[i], NN)

    groups(rows, restrict)
    piece_copies = []
    for o in range(n - 1):
        for k in range(cap):
            i = 2 * idx[item_at + o * cap + k] + 1
            piece_send[o, pl.ds(k, 1), :] = mate_rows[pl.ds(i, 1), :]
        piece_copies.append(to_peer(5, o, piece_send.at[o], piece_recv.at[o]))
        piece_copies[-1].start()

    for copy in p_copies:
        copy.wait()
    for copy in b_copies:
        copy.wait()

    def products(g, carry):
        for r in range(4):
            c = 4 * g + r
            slot = idx[recv_at + c]
            block = v_prol[2 * c]
            upper = dot(block, v_diag[2 * c], TN).astype(BF)
            across = dot(block, v_pair[2 * c], TN).astype(BF)
            total = dot(upper, block, NN)
            total = total + dot(across, recv_p[slot // cap, slot % cap], NN)
            pre[c] = total + dot(recv_b[slot // cap, slot % cap], block, NN)
        return carry

    lax.fori_loop(0, half // 4, products, 0)

    for copy in piece_copies:
        copy.wait()

    def restricted(g, carry):
        for r in range(8):
            c = g * 8 + r
            slot = idx[recv_at + c]
            piece = piece_recv[slot // cap, pl.ds(slot % cap, 1), :]
            restr[pl.ds(c, 1), :] = mate_rows[pl.ds(2 * c, 1), :] + piece
        return carry

    lax.fori_loop(0, half // 8, restricted, 0)
    rest_out[...] = restr[...]

    for copy in i_copies:
        copy.wait()

    def finish(first):
        at = pl.ds(first, 8)
        value = restr[at, :]
        start = THETA * value
        both = two_parts(start)
        moved = jnp.zeros((8, 128), F32)
        for r in range(8):
            slot = idx[recv_at + first + r]
            last = recv_i[slot // cap, slot % cap].astype(F32)
            made = (pre[first + r] + last).astype(BF)
            out_blocks[first + r] = made
            part = dot(both, made, NT)
            moved = jnp.where(row_id == r, part[:8] + part[8:], moved)
        corr[at, :] = start + THETA * (value - moved)

    groups(half, finish)
    store = pltpu.make_async_copy(out_blocks, h_blocks, load_sems.at[5])
    store.start()
    back_copies = []
    for o in range(n - 1):
        for k in range(cap):
            c = idx[back_at + o * cap + k]
            back_send[o, pl.ds(k, 1), :] = corr[pl.ds(c, 1), :]
        back_copies.append(to_peer(6, o, back_send.at[o], back_recv.at[o], back=True))
        back_copies[-1].start()

    def lift_even(first):
        at = pl.ds(first, 8)
        odd_corr[at, :] = exact_rows(corr[at, :], first, lambda c: v_prol[2 * c], NT)
        for r in range(8):
            i = 2 * (first + r)
            fine_out[pl.ds(i, 1), :] = iterate[pl.ds(i, 1), :] + odd_corr[pl.ds(first + r, 1), :]

    groups(half, lift_even)
    for copy in back_copies:
        copy.wait()

    def take_back(g, carry):
        for r in range(8):
            j = g * 8 + r
            slot = idx[send_at + j]
            odd_corr[pl.ds(j, 1), :] = back_recv[slot // cap, pl.ds(slot % cap, 1), :]
        return carry

    lax.fori_loop(0, half // 8, take_back, 0)

    def lift_odd(first):
        at = pl.ds(first, 8)
        corr[at, :] = exact_rows(odd_corr[at, :], first, lambda j: v_prol[2 * j + 1], NT)
        for r in range(8):
            i = 2 * (first + r) + 1
            fine_out[pl.ds(i, 1), :] = iterate[pl.ds(i, 1), :] + corr[pl.ds(first + r, 1), :]

    groups(half, lift_odd)
    store.wait()


def hand_over(fine, blocks, rest, fine_out, blocks_out, rest_out):
    fine_out[...] = fine[...]
    blocks_out[...] = blocks[...]
    rest_out[...] = rest[...]


def tables(n, m, cap, rows, col_index, partner, odd_owner):
    half = rows // 2
    slots = (n - 1) * cap
    line = lax.axis_index("rx")
    col = lax.axis_index("ry")
    mate = jnp.stack([partner, 2 * odd_owner], axis=1).reshape(rows)

    def line_slot(row):
        return (line - row // rows // m) % n * rows + row % rows

    below = (col_index[:, 1] // rows) % m == (col - 1) % m
    side = jnp.where(below, 0, rows) + col_index[:, 1] % rows
    order = jnp.arange(half, dtype=jnp.int32)

    def slot_of(offset, key):
        same = offset[:, None] == offset[None, :]
        rank = jnp.sum(same & (key[None, :] < key[:, None]), axis=1, dtype=jnp.int32)
        return (offset - 1) * cap + rank

    send = slot_of((odd_owner // half // m - line) % n, odd_owner)
    recv = slot_of((line - partner // rows // m) % n, order)

    def inverse(slot):
        hits = slot[None, :] == jnp.arange(slots, dtype=jnp.int32)[:, None]
        return jnp.sum(jnp.where(hits, order[None, :], 0), axis=1, dtype=jnp.int32)

    return jnp.concatenate(
        [line_slot(mate), line_slot(col_index[:, 0]), side, recv, send, inverse(send), inverse(recv)]
    )


def body(n, m, rhs, a_diag, a_pair, a_far, approx_inv, prolong, col_index, partner, odd_owner):
    rows, width = rhs.shape
    half = rows // 2
    cap = half // (n // 2)
    idx = tables(n, m, cap, rows, col_index, partner, odd_owner)
    vmem = pl.BlockSpec(memory_space=pltpu.VMEM)
    hbm = pl.BlockSpec(memory_space=pl.ANY)
    block = (width, width)
    slot_blocks = pltpu.VMEM((n - 1, cap) + block, BF)
    row_vals = pltpu.VMEM((rows, width), F32)
    half_vals = pltpu.VMEM((half, width), F32)
    slot_vals = pltpu.VMEM((n - 1, cap, width), F32)
    row_blocks = pltpu.VMEM((rows,) + block, BF)
    dma = pltpu.SemaphoreType.DMA
    fine, blocks, restricted = pl.pallas_call(
        functools.partial(kernel, n, m, cap, rows),
        out_shape=(
            jax.ShapeDtypeStruct((rows, width), F32),
            jax.ShapeDtypeStruct((half,) + block, BF),
            jax.ShapeDtypeStruct((half, width), F32),
        ),
        in_specs=[pl.BlockSpec(memory_space=pltpu.SMEM), vmem] + [hbm] * 5,
        out_specs=(vmem, hbm, vmem),
        scratch_shapes=[
            row_blocks,
            row_blocks,
            pltpu.VMEM((rows, 2) + block, BF),
            row_blocks,
            row_blocks,
            pltpu.VMEM((half,) + block, BF),
            slot_blocks,
            slot_blocks,
            slot_blocks,
            slot_blocks,
            slot_blocks,
            slot_blocks,
            pltpu.VMEM((half,) + block, F32),
            pltpu.VMEM((2, rows, width), BF),
            pltpu.VMEM((2, n - 1, rows, width), BF),
            pltpu.VMEM((2, 2, rows, width), BF),
            pltpu.VMEM((n, rows, width), F32),
            pltpu.VMEM((2, rows, width), F32),
            row_vals,
            row_vals,
            row_vals,
            row_vals,
            row_vals,
            half_vals,
            half_vals,
            half_vals,
            slot_vals,
            slot_vals,
            slot_vals,
            slot_vals,
            dma((6,)),
            dma((7, n)),
            dma((7, n)),
            dma((2, 2)),
            dma((2, 2)),
        ],
        compiler_params=pltpu.CompilerParams(
            collective_id=0, has_side_effects=True, vmem_limit_bytes=61 * 1024 * 1024
        ),
    )(idx, rhs, a_diag, a_pair, a_far, approx_inv, prolong)
    steps = 4
    parts = [
        pl.BlockSpec((rows // steps, width), lambda i: (i, 0)),
        pl.BlockSpec((half // steps,) + block, lambda i: (i, 0, 0)),
        pl.BlockSpec((half // steps, width), lambda i: (i, 0)),
    ]
    return pl.pallas_call(
        hand_over,
        grid=(steps,),
        out_shape=[jax.ShapeDtypeStruct(a.shape, a.dtype) for a in (fine, blocks, restricted)],
        in_specs=parts,
        out_specs=parts,
        compiler_params=pltpu.CompilerParams(vmem_limit_bytes=16 * 1024 * 1024),
    )(fine, blocks, restricted)


def solution(mesh):
    n, m = mesh.shape["rx"], mesh.shape["ry"]
    return jax.shard_map(
        functools.partial(body, n, m),
        mesh=mesh,
        in_specs=(
            P(("rx", "ry"), None),
            P(("rx", "ry"), None, None),
            P(("rx", "ry"), None, None),
            P(("rx", "ry"), None, None, None),
            P(("rx", "ry"), None, None),
            P(("rx", "ry"), None, None),
            P(("rx", "ry"), None),
            P(("rx", "ry")),
            P(("rx", "ry")),
        ),
        out_specs=(P(("rx", "ry"), None), P(("rx", "ry"), None, None), P(("rx", "ry"), None)),
        check_vma=False,
    )
```

```python
import functools

import jax
import jax.numpy as jnp
from jax import lax
from jax.experimental import pallas as pl
from jax.experimental.pallas import tpu as pltpu
from jax.sharding import PartitionSpec as P

OMEGA = 0.7
THETA = 0.08
MESH = pl.DeviceIdType.MESH
BF = jnp.bfloat16
F32 = jnp.float32

NT = (((1,), (1,)), ((), ()))
NN = (((1,), (0,)), ((), ()))
TN = (((0,), (0,)), ((), ()))


def dot(left, right, dims):
    return lax.dot_general(left, right, dims, preferred_element_type=F32)


def two_parts(values):
    high = values.astype(BF)
    low = (values - high.astype(F32)).astype(BF)
    return jnp.concatenate([high, low], axis=0)


def kernel(
    n,
    m,
    cap,
    rows,
    idx,
    rhs,
    h_diag,
    h_pair,
    h_far,
    h_inv,
    h_prol,
    fine_out,
    h_blocks,
    rest_out,
    v_diag,
    v_pair,
    v_far,
    v_inv,
    v_prol,
    out_blocks,
    send_p,
    send_b,
    send_i,
    recv_p,
    recv_b,
    recv_i,
    pre,
    it_send,
    it_recv,
    side_recv,
    line_vals,
    side_vals,
    mate_rows,
    far_rows,
    side_rows,
    iterate,
    defect,
    restr,
    corr,
    odd_corr,
    piece_send,
    piece_recv,
    back_send,
    back_recv,
    load_sems,
    s_sems,
    r_sems,
    ss_sems,
    sr_sems,
):
    half = rows // 2
    slots = (n - 1) * cap
    mate_at, far_at, side_at = 0, rows, 2 * rows
    recv_at = 3 * rows
    send_at = recv_at + half
    item_at = send_at + half
    back_at = item_at + slots
    line = lax.axis_index("rx")
    col = lax.axis_index("ry")
    peers = [lax.rem(line + o, n) for o in range(1, n)]
    back_peers = [lax.rem(line + n - o, n) for o in range(1, n)]
    below, above = lax.rem(col + m - 1, m), lax.rem(col + 1, m)

    loads = [
        pltpu.make_async_copy(src, dst, load_sems.at[i])
        for i, (src, dst) in enumerate(
            [(h_prol, v_prol), (h_inv, v_inv), (h_pair, v_pair), (h_diag, v_diag), (h_far, v_far)]
        )
    ]
    for load in loads:
        load.start()

    barrier = pltpu.get_barrier_semaphore()
    for peer in peers:
        pl.semaphore_signal(barrier, inc=1, device_id=(peer, col), device_id_type=MESH)
    for side in (below, above):
        pl.semaphore_signal(barrier, inc=1, device_id=(line, side), device_id_type=MESH)
    def to_peer(kind, o, src, dst, back=False):
        return pltpu.make_async_remote_copy(
            src_ref=src,
            dst_ref=dst,
            send_sem=s_sems.at[kind, o],
            recv_sem=r_sems.at[kind, o],
            device_id=((back_peers if back else peers)[o], col),
            device_id_type=MESH,
        )

    turn_to = 1 - 2 * lax.rem(line, 2)
    twin = line + turn_to

    def iterate_copy(turn, src, dst_at, sem_at, peer):
        return pltpu.make_async_remote_copy(
            src_ref=src,
            dst_ref=it_recv.at[turn, dst_at],
            send_sem=s_sems.at[turn, sem_at],
            recv_sem=r_sems.at[turn, dst_at],
            device_id=(peer, col),
            device_id_type=MESH,
        )

    twin_at = lax.rem(turn_to + n, n) - 1
    twin_from = lax.rem(n - turn_to, n) - 1

    def send_iterate(turn):
        copies = [iterate_copy(turn, it_send.at[turn], twin_at, 0, twin)]
        for o in range(2, n, 2):
            copies.append(iterate_copy(turn, it_send.at[turn], o - 1, o - 1, peers[o - 1]))
        for k, side in enumerate((above, below)):
            copies.append(
                pltpu.make_async_remote_copy(
                    src_ref=it_send.at[turn],
                    dst_ref=side_recv.at[turn, k],
                    send_sem=ss_sems.at[turn, k],
                    recv_sem=sr_sems.at[turn, k],
                    device_id=(line, side),
                    device_id_type=MESH,
                )
            )
        for copy in copies:
            copy.start()
        return copies

    def take_iterates(turn, copies):
        passed = []
        for o in range(2, n, 2):
            copies[o // 2].wait_recv()
            dst_at = lax.rem(o + turn_to + n, n) - 1
            passed.append(iterate_copy(turn, it_recv.at[turn, o - 1], dst_at, o, twin))
            passed[-1].start()
        for copy in copies:
            copy.wait_send()
        for copy in copies[n // 2 :]:
            copy.wait_recv()
        iterate_copy(turn, it_send.at[turn], twin_from, 0, twin).wait_recv()
        for o in range(2, n, 2):
            source_at = lax.rem(o - turn_to + n, n) - 1
            iterate_copy(turn, it_send.at[turn], source_at, o, twin).wait_recv()
        for copy in passed:
            copy.wait_send()

    row_id = lax.broadcasted_iota(jnp.int32, (8, 128), 0)

    def groups(count, body):
        def step(g, carry):
            body(pl.multiple_of(g * 8, 8))
            return carry

        lax.fori_loop(0, count // 8, step, 0)

    def exact_rows(values, first, matrix, dims):
        both = two_parts(values)
        total = jnp.zeros((8, 128), F32)
        for r in range(8):
            part = dot(both, matrix(first + r), dims)
            total = jnp.where(row_id == r, part[:8] + part[8:], total)
        return total

    def gather_rows(turn):
        line_vals[0] = it_send[turn].astype(F32)
        for o in range(n - 1):
            line_vals[o + 1] = it_recv[turn, o].astype(F32)
        side_vals[...] = side_recv[turn].astype(F32)

        def step(g, carry):
            for r in range(8):
                i = g * 8 + r
                a = idx[mate_at + (r % 2) * half + g * 4 + r // 2]
                b = idx[far_at + i]
                c = idx[side_at + i]
                mate_rows[pl.ds(i, 1), :] = line_vals[a // rows, pl.ds(a % rows, 1), :]
                far_rows[pl.ds(i, 1), :] = line_vals[b // rows, pl.ds(b % rows, 1), :]
                side_rows[pl.ds(i, 1), :] = side_vals[c // rows, pl.ds(c % rows, 1), :]
            return carry

        lax.fori_loop(0, rows // 8, step, 0)

    def subtract_operator():
        def body(first):
            at = pl.ds(first, 8)
            own = two_parts(iterate[at, :])
            mates = mate_rows[at, :].astype(BF)
            fars = far_rows[at, :].astype(BF)
            sides = side_rows[at, :].astype(BF)
            total = jnp.zeros((8, 128), F32)
            for r in range(8):
                i = first + r
                main = dot(own, v_diag[i], NT)
                part = main[:8] + main[8:] + dot(mates, v_pair[i], NT)
                part = part + dot(fars, v_far[i, 0], NT) + dot(sides, v_far[i, 1], NT)
                total = jnp.where(row_id == r, part, total)
            defect[at, :] = rhs[at, :] - total

        groups(rows, body)

    loads[0].wait()
    pl.semaphore_wait(barrier, n + 1)
    p_copies = []
    for o in range(n - 1):

        def pack(k, carry):
            for r in range(4):
                send_p[o, 4 * k + r] = v_prol[2 * idx[item_at + o * cap + 4 * k + r] + 1]
            return carry

        lax.fori_loop(0, cap // 4, pack, 0)
        p_copies.append(to_peer(2, o, send_p.at[o], recv_p.at[o]))
        p_copies[-1].start()

    loads[1].wait()

    def first_sweep(first):
        at = pl.ds(first, 8)
        iterate[at, :] = OMEGA * exact_rows(rhs[at, :], first, lambda i: v_inv[i], NT)

    groups(rows, first_sweep)
    it_send[0] = iterate[...].astype(BF)
    it_copies = send_iterate(0)

    loads[2].wait()
    b_copies = []
    for o in range(n - 1):

        def behind(k, carry):
            for r in range(4):
                i = 2 * idx[item_at + o * cap + 4 * k + r] + 1
                send_b[o, 4 * k + r] = dot(v_prol[i], v_pair[i], TN).astype(BF)
            return carry

        lax.fori_loop(0, cap // 4, behind, 0)
        b_copies.append(to_peer(3, o, send_b.at[o], recv_b.at[o]))
        b_copies[-1].start()

    for load in loads[3:]:
        load.wait()
    take_iterates(0, it_copies)
    gather_rows(0)
    subtract_operator()

    def second_sweep(first):
        at = pl.ds(first, 8)
        step = exact_rows(defect[at, :], first, lambda i: v_inv[i], NT)
        iterate[at, :] = iterate[at, :] + OMEGA * step

    groups(rows, second_sweep)
    it_send[1] = iterate[...].astype(BF)
    it_copies = send_iterate(1)

    i_copies = []
    for o in range(n - 1):

        def inner(k, carry):
            for r in range(4):
                i = 2 * idx[item_at + o * cap + 4 * k + r] + 1
                block = v_prol[i]
                lower = dot(block, v_diag[i], TN).astype(BF)
                send_i[o, 4 * k + r] = dot(lower, block, NN).astype(BF)
            return carry

        lax.fori_loop(0, cap // 4, inner, 0)
        i_copies.append(to_peer(4, o, send_i.at[o], recv_i.at[o]))
        i_copies[-1].start()

    take_iterates(1, it_copies)
    gather_rows(1)
    subtract_operator()

    def restrict(first):
        at = pl.ds(first, 8)
        mate_rows[at, :] = exact_rows(defect[at, :], first, lambda i: v_prol[i], NN)

    groups(rows, restrict)
    piece_copies = []
    for o in range(n - 1):
        for k in range(cap):
            i = 2 * idx[item_at + o * cap + k] + 1
            piece_send[o, pl.ds(k, 1), :] = mate_rows[pl.ds(i, 1), :]
        piece_copies.append(to_peer(5, o, piece_send.at[o], piece_recv.at[o]))
        piece_copies[-1].start()

    for copy in p_copies:
        copy.wait()
    for copy in b_copies:
        copy.wait()

    def products(g, carry):
        for r in range(4):
            c = 4 * g + r
            slot = idx[recv_at + c]
            block = v_prol[2 * c]
            upper = dot(block, v_diag[2 * c], TN).astype(BF)
            across = dot(block, v_pair[2 * c], TN).astype(BF)
            total = dot(upper, block, NN)
            total = total + dot(across, recv_p[slot // cap, slot % cap], NN)
            pre[c] = total + dot(recv_b[slot // cap, slot % cap], block, NN)
        return carry

    lax.fori_loop(0, half // 4, products, 0)

    for copy in piece_copies:
        copy.wait()

    def restricted(g, carry):
        for r in range(8):
            c = g * 8 + r
            slot = idx[recv_at + c]
            piece = piece_recv[slot // cap, pl.ds(slot % cap, 1), :]
            restr[pl.ds(c, 1), :] = mate_rows[pl.ds(2 * c, 1), :] + piece
        return carry

    lax.fori_loop(0, half // 8, restricted, 0)
    rest_out[...] = restr[...]

    for copy in i_copies:
        copy.wait()

    def finish(first):
        at = pl.ds(first, 8)
        value = restr[at, :]
        start = THETA * value
        both = two_parts(start)
        moved = jnp.zeros((8, 128), F32)
        for r in range(8):
            slot = idx[recv_at + first + r]
            last = recv_i[slot // cap, slot % cap].astype(F32)
            made = (pre[first + r] + last).astype(BF)
            out_blocks[first + r] = made
            part = dot(both, made, NT)
            moved = jnp.where(row_id == r, part[:8] + part[8:], moved)
        corr[at, :] = start + THETA * (value - moved)

    groups(half, finish)
    store = pltpu.make_async_copy(out_blocks, h_blocks, load_sems.at[5])
    store.start()
    back_copies = []
    for o in range(n - 1):
        for k in range(cap):
            c = idx[back_at + o * cap + k]
            back_send[o, pl.ds(k, 1), :] = corr[pl.ds(c, 1), :]
        back_copies.append(to_peer(6, o, back_send.at[o], back_recv.at[o], back=True))
        back_copies[-1].start()

    def lift_even(first):
        at = pl.ds(first, 8)
        odd_corr[at, :] = exact_rows(corr[at, :], first, lambda c: v_prol[2 * c], NT)
        for r in range(8):
            i = 2 * (first + r)
            fine_out[pl.ds(i, 1), :] = iterate[pl.ds(i, 1), :] + odd_corr[pl.ds(first + r, 1), :]

    groups(half, lift_even)
    for copy in back_copies:
        copy.wait()

    def take_back(g, carry):
        for r in range(8):
            j = g * 8 + r
            slot = idx[send_at + j]
            odd_corr[pl.ds(j, 1), :] = back_recv[slot // cap, pl.ds(slot % cap, 1), :]
        return carry

    lax.fori_loop(0, half // 8, take_back, 0)

    def lift_odd(first):
        at = pl.ds(first, 8)
        corr[at, :] = exact_rows(odd_corr[at, :], first, lambda j: v_prol[2 * j + 1], NT)
        for r in range(8):
            i = 2 * (first + r) + 1
            fine_out[pl.ds(i, 1), :] = iterate[pl.ds(i, 1), :] + corr[pl.ds(first + r, 1), :]

    groups(half, lift_odd)
    store.wait()


def hand_over(fine, blocks, rest, fine_out, blocks_out, rest_out):
    fine_out[...] = fine[...]
    blocks_out[...] = blocks[...]
    rest_out[...] = rest[...]


def tables(n, m, cap, rows, col_index, partner, odd_owner):
    half = rows // 2
    slots = (n - 1) * cap
    line = lax.axis_index("rx")
    col = lax.axis_index("ry")

    def line_slot(row):
        return (line - row // rows // m) % n * rows + row % rows

    below = (col_index[:, 1] // rows) % m == (col - 1) % m
    side = jnp.where(below, 0, rows) + col_index[:, 1] % rows
    order = jnp.arange(half, dtype=jnp.int32)

    def slot_of(offset, key):
        same = offset[:, None] == offset[None, :]
        rank = jnp.sum(same & (key[None, :] < key[:, None]), axis=1, dtype=jnp.int32)
        return (offset - 1) * cap + rank

    send = slot_of((odd_owner // half // m - line) % n, odd_owner)
    recv = slot_of((line - partner // rows // m) % n, order)

    def inverse(slot):
        hits = slot[None, :] == jnp.arange(slots, dtype=jnp.int32)[:, None]
        return jnp.sum(jnp.where(hits, order[None, :], 0), axis=1, dtype=jnp.int32)

    return jnp.concatenate(
        [
            line_slot(partner),
            line_slot(2 * odd_owner),
            line_slot(col_index[:, 0]),
            side,
            recv,
            send,
            inverse(send),
            inverse(recv),
        ]
    )


def body(n, m, rhs, a_diag, a_pair, a_far, approx_inv, prolong, col_index, partner, odd_owner):
    rows, width = rhs.shape
    half = rows // 2
    cap = half // (n // 2)
    idx = tables(n, m, cap, rows, col_index, partner, odd_owner)
    vmem = pl.BlockSpec(memory_space=pltpu.VMEM)
    hbm = pl.BlockSpec(memory_space=pl.ANY)
    block = (width, width)
    slot_blocks = pltpu.VMEM((n - 1, cap) + block, BF)
    row_vals = pltpu.VMEM((rows, width), F32)
    half_vals = pltpu.VMEM((half, width), F32)
    slot_vals = pltpu.VMEM((n - 1, cap, width), F32)
    row_blocks = pltpu.VMEM((rows,) + block, BF)
    dma = pltpu.SemaphoreType.DMA
    fine, blocks, restricted = pl.pallas_call(
        functools.partial(kernel, n, m, cap, rows),
        out_shape=(
            jax.ShapeDtypeStruct((rows, width), F32),
            jax.ShapeDtypeStruct((half,) + block, BF),
            jax.ShapeDtypeStruct((half, width), F32),
        ),
        in_specs=[pl.BlockSpec(memory_space=pltpu.SMEM), vmem] + [hbm] * 5,
        out_specs=(vmem, hbm, vmem),
        scratch_shapes=[
            row_blocks,
            row_blocks,
            pltpu.VMEM((rows, 2) + block, BF),
            row_blocks,
            row_blocks,
            pltpu.VMEM((half,) + block, BF),
            slot_blocks,
            slot_blocks,
            slot_blocks,
            slot_blocks,
            slot_blocks,
            slot_blocks,
            pltpu.VMEM((half,) + block, F32),
            pltpu.VMEM((2, rows, width), BF),
            pltpu.VMEM((2, n - 1, rows, width), BF),
            pltpu.VMEM((2, 2, rows, width), BF),
            pltpu.VMEM((n, rows, width), F32),
            pltpu.VMEM((2, rows, width), F32),
            row_vals,
            row_vals,
            row_vals,
            row_vals,
            row_vals,
            half_vals,
            half_vals,
            half_vals,
            slot_vals,
            slot_vals,
            slot_vals,
            slot_vals,
            dma((6,)),
            dma((7, n)),
            dma((7, n)),
            dma((2, 2)),
            dma((2, 2)),
        ],
        compiler_params=pltpu.CompilerParams(
            collective_id=0, has_side_effects=True, vmem_limit_bytes=61 * 1024 * 1024
        ),
    )(idx, rhs, a_diag, a_pair, a_far, approx_inv, prolong)
    steps = 4
    parts = [
        pl.BlockSpec((rows // steps, width), lambda i: (i, 0)),
        pl.BlockSpec((half // steps,) + block, lambda i: (i, 0, 0)),
        pl.BlockSpec((half // steps, width), lambda i: (i, 0)),
    ]
    return pl.pallas_call(
        hand_over,
        grid=(steps,),
        out_shape=[jax.ShapeDtypeStruct(a.shape, a.dtype) for a in (fine, blocks, restricted)],
        in_specs=parts,
        out_specs=parts,
        compiler_params=pltpu.CompilerParams(vmem_limit_bytes=61 * 1024 * 1024),
    )(fine, blocks, restricted)


def solution(mesh):
    n, m = mesh.shape["rx"], mesh.shape["ry"]
    return jax.shard_map(
        functools.partial(body, n, m),
        mesh=mesh,
        in_specs=(
            P(("rx", "ry"), None),
            P(("rx", "ry"), None, None),
            P(("rx", "ry"), None, None),
            P(("rx", "ry"), None, None, None),
            P(("rx", "ry"), None, None),
            P(("rx", "ry"), None, None),
            P(("rx", "ry"), None),
            P(("rx", "ry")),
            P(("rx", "ry")),
        ),
        out_specs=(P(("rx", "ry"), None), P(("rx", "ry"), None, None), P(("rx", "ry"), None)),
        check_vma=False,
    )
```
